256 devices in a mesh: ctx: 32 (over z, x), head: 8 (over y, core).
Axes of the slice: x: 4, y: 4, z: 8, core: 2. Of those that a mesh axis runs over, the one named last changes fastest.
Arguments:
- query_rows: bfloat16 [32768, 16, 128], P(('ctx', 'head')), may hold values from -6 to 6
- key_rows: bfloat16 [32768, 16, 128], P(('ctx', 'head')), may hold values from -4 to 4
- value_rows: bfloat16 [32768, 32, 128], P(('ctx', 'head')), may hold values from -6 to 6
- beta_rows: bfloat16 [32768, 32], P(('ctx', 'head')), may hold values from 0.0099 to 0.5
- log_gate: bfloat16 [32768, 32], P(('ctx', 'head')), may hold values from -0.75 to 0
Outputs:
- mixed_values: bfloat16 [32768, 32, 128], P(('ctx', 'head'))
The draws below stay inside these ranges and needn't reach their ends.
All inputs are finite; a program needn't handle non-finite values.
Results may differ from the reference program's by a relative error of at most 0.0013.
Values may be sent and summed in bfloat16 or wider, within the bound.
No kernel may reach another device: no remote copies, remote signals or barrier semaphores. Data moves between devices by JAX's collectives and lax.ppermute only.
A program may use at most 128 MiB of HBM per device.

```python
import math
import jax
import jax.numpy as jnp
from jax import lax

HK = 16
VALUE_HEADS = 32
DK = 128
DV = 128
BLK = 128
TOK_CTX = 1024
SEQUENCE_TOKENS = 32768


def draw_log_gate(key, part):
    every_key = jax.random.split(key, 6)
    fast_share = 0.5
    fast_heads = jax.random.bernoulli(every_key[0], fast_share, (VALUE_HEADS,))
    fast_rate = jnp.exp(jax.random.uniform(every_key[1], (VALUE_HEADS,), jnp.float32, math.log(1.0 / 50.0), math.log(1.0 / 30.0)))
    span_count = SEQUENCE_TOKENS // TOK_CTX
    span_factor = jnp.exp(jax.random.uniform(every_key[2], (span_count, VALUE_HEADS), jnp.float32, math.log(0.5), math.log(2.0)))
    span_factor = jnp.repeat(span_factor, TOK_CTX, axis=0)
    slow_rate = 0.1 * math.log(10.0) / SEQUENCE_TOKENS * span_factor
    roughness = jax.random.uniform(every_key[3], (SEQUENCE_TOKENS, VALUE_HEADS), jnp.float32, 0.5, 1.5)
    forget_speed = jnp.where(fast_heads[None, :], fast_rate[None, :], slow_rate) * roughness
    spike_locations = jax.random.permutation(every_key[4], SEQUENCE_TOKENS)[:3]
    spike_penalty = jax.random.uniform(every_key[5], (3, VALUE_HEADS), jnp.float32, 0.5, 0.8)
    token_places = jnp.arange(SEQUENCE_TOKENS)
    spike_matches = (token_places[:, None] == spike_locations[None, :]).astype(jnp.float32)
    spike_events = jnp.sum(spike_matches[:, :, None] * jnp.log(spike_penalty)[None, :, :], axis=1)
    return (spike_events - forget_speed).astype(jnp.bfloat16)


def draw_key_rows(key, part):
    every_key = jax.random.split(jax.random.fold_in(key, 11), 2)
    shared = jax.random.normal(every_key[0], (HK, DK), jnp.float32)
    noise = jax.random.normal(every_key[1], (SEQUENCE_TOKENS, HK, DK), jnp.float32)
    return jnp.clip(0.85 * shared[None, :, :] + 0.53 * noise, -4.0, 4.0).astype(jnp.bfloat16)


def draw_beta_rows(key, part):
    every_key = jax.random.split(jax.random.fold_in(key, 23), 3)
    base = jnp.exp(jax.random.uniform(every_key[0], (SEQUENCE_TOKENS, VALUE_HEADS), jnp.float32, math.log(0.01), math.log(0.04)))
    block_total = SEQUENCE_TOKENS // BLK
    strong_blocks = jax.random.bernoulli(every_key[1], 1.0 / 32.0, (block_total, VALUE_HEADS))
    strong_blocks = jnp.repeat(strong_blocks, BLK, axis=0)
    strong = jax.random.uniform(every_key[2], (SEQUENCE_TOKENS, VALUE_HEADS), jnp.float32, 0.25, 0.5)
    return jnp.where(strong_blocks, strong, base).astype(jnp.bfloat16)


def steps_of(rng, extent, cuts, least, top_value):
    gain = 1.0
    for dim, blocks in cuts:
        steps = jax.random.uniform(jax.random.fold_in(jax.random.fold_in(rng, 6), dim), (blocks,), jnp.float32, least / len(cuts), top_value / len(cuts))
        gain = gain * jnp.repeat(jnp.exp(steps), extent[dim] // blocks).reshape((-1,) + (1,) * (len(extent) - 1 - dim))
    return gain


def gaussian(key, extent, scale, most, cuts=(), kind=jnp.bfloat16):
    level = steps_of(key, extent, cuts, -0.22, 0.18) if cuts else 1.0
    result = jax.random.normal(key, extent, jnp.float32) * scale * level
    return jnp.minimum(jnp.maximum(result, -most), most).astype(kind)


def setup_inputs(seed: int = 0) -> dict:
    key_list = jax.random.split(jax.random.key(seed), 6)
    return {
        "query_rows": gaussian(key_list[0], (SEQUENCE_TOKENS, HK, DK), 1.0, 6.0, ((0, 256),)),
        "key_rows": draw_key_rows(jax.random.fold_in(key_list[5], 71), 0),
        "value_rows": gaussian(key_list[2], (SEQUENCE_TOKENS, VALUE_HEADS, DV), 1.0, 6.0, ((0, 256),)),
        "beta_rows": draw_beta_rows(jax.random.fold_in(key_list[5], 71), 0),
        "log_gate": draw_log_gate(jax.random.fold_in(key_list[5], 71), 0),
    }


def unit_rows(source):
    widened = source.astype(jnp.float32)
    return widened * lax.rsqrt(lax.optimization_barrier(jnp.sum(widened * widened, -1, keepdims=True)) + 1e-06)

def sweep_blocks(initial, key_unit, queries, values, beta_vals, gate_logs, with_values, with_output):
    total_rows, head_count = gate_logs.shape
    block_count = total_rows // BLK
    row_total = initial.shape[1]
    split_at = row_total - DV
    token_places = jnp.arange(BLK)
    strict_lower = token_places[:, None] > token_places[None, :]
    inclusive = token_places[:, None] >= token_places[None, :]
    identity_block = jnp.eye(BLK, dtype=jnp.float32)
    highest = lax.Precision.HIGHEST

    def advance(carried, pieces):
        key_block, query_block, value_block, beta_block, gate_block = pieces
        cumulative = jnp.cumsum(gate_block, axis=0)
        cumul_heads = cumulative.T
        spread = jnp.minimum(cumul_heads[:, :, None] - cumul_heads[:, None, :], 0.0)
        decay_table = jnp.exp(spread)
        key_gram = jnp.einsum('chd,jhd->hcj', key_block, key_block, precision=highest)
        lower_part = jnp.where(strict_lower, beta_block.T[:, :, None] * decay_table * key_gram, 0.0)
        system = identity_block + lower_part
        growth = jnp.exp(cumul_heads)
        projected = jnp.einsum('chd,hrd->hcr', key_block, carried, precision=highest)
        right_side = -(beta_block.T * growth)[:, :, None] * projected
        if with_values:
            written = jnp.einsum('ch,chv->hcv', beta_block, value_block, precision=highest)
            right_side = jnp.concatenate([right_side[..., :split_at], right_side[..., split_at:] + written], -1)
        errors = jax.vmap(lambda mat, rhs_part: jax.scipy.linalg.solve_triangular(mat, rhs_part, lower=True, unit_diagonal=True))(system, right_side)
        last_log = cumul_heads[:, -1]
        weights = jnp.exp(last_log[None, :] - cumulative)
        updated = jnp.exp(last_log)[:, None, None] * carried + jnp.einsum('hcr,chd->hrd', errors, key_block * weights[:, :, None], precision=highest)
        emitted = None
        if with_output:
            live_rows = carried[:, split_at:]
            carried_term = jnp.einsum('chd,hvd->chv', query_block, live_rows, precision=highest)
            scores = jnp.einsum('chd,jhd->hcj', query_block, key_block, precision=highest)
            masked_scores = jnp.where(inclusive, scores * decay_table, 0.0)
            emitted = growth.T[:, :, None] * carried_term + jnp.einsum('hcj,hjv->chv', masked_scores, errors[..., split_at:], precision=highest)
        return (updated, emitted)

    def blocked(source):
        return source.reshape((block_count, BLK) + source.shape[1:])
    query_src = key_unit if queries is None else queries
    final_pairs, emitted_all = lax.scan(advance, initial, (blocked(key_unit), blocked(query_src), blocked(values), blocked(beta_vals), blocked(gate_logs)))
    if with_output:
        emitted_all = emitted_all.reshape(total_rows, head_count, DV)
    return (final_pairs, emitted_all)

def reference(query_rows, key_rows, value_rows, beta_rows, log_gate):
    group_ratio = VALUE_HEADS // HK
    key_unit = jnp.repeat(unit_rows(key_rows), group_ratio, axis=1)
    query_unit = jnp.repeat(unit_rows(query_rows), group_ratio, axis=1) * DK ** (-0.5)
    initial = jnp.zeros((VALUE_HEADS, DV, DK), jnp.float32)
    final_pairs, outputs = sweep_blocks(initial, key_unit, query_unit, value_rows.astype(jnp.float32), beta_rows.astype(jnp.float32), log_gate.astype(jnp.float32), True, True)
    return outputs.astype(jnp.bfloat16)
```

```python
import jax
import jax.numpy as jnp
from jax import lax
from jax.experimental import pallas as pl
from jax.experimental.pallas import tpu as pltpu
from jax.sharding import PartitionSpec as P

N = 128
HEADS = 4
KEYS = 2
BLOCKS = 8
ROWS = 1040
Q0, V0, G0 = KEYS * N, 2 * KEYS * N, 2 * KEYS * N + HEADS * N
STEP = 2
F32, BF16 = jnp.float32, jnp.bfloat16


def iota(shape, dim):
    return lax.broadcasted_iota(jnp.int32, shape, dim)


def split(x):
    hi = x.astype(BF16)
    return hi, (x - hi.astype(F32)).astype(BF16)


def dot(a, b):
    return jnp.dot(a, b, preferred_element_type=F32)


def dot_nt(a, b):
    return lax.dot_general(a, b, (((1,), (1,)), ((), ())), preferred_element_type=F32)


def dot_tn(a, b):
    return lax.dot_general(a, b, (((0,), (0,)), ((), ())), preferred_element_type=F32)


def left(a):
    hi, lo = a
    return jnp.concatenate([hi, lo, hi, lo], axis=1)


def right(b):
    hi, lo = b
    return jnp.concatenate([hi, hi, lo, lo], axis=0)


def dot4(a, b):
    return dot(left(a), right(b))


def gate_rows(gates):
    upper = (iota((N, N), 0) <= iota((N, N), 1)).astype(F32).astype(BF16)
    return dot(gates, upper)


def gate_columns(gates):
    lower = (iota((N, N), 0) >= iota((N, N), 1)).astype(F32).astype(BF16)
    eye = (iota((N, N), 0) == iota((N, N), 1)).astype(F32).astype(BF16)
    both = dot_nt(jnp.concatenate([lower, eye], axis=0), gates)
    return both[:N], both[N:]


def small_inverses(lower_parts):
    count = len(lower_parts)
    group = iota((16, N), 1) // 16
    rows = []
    for part in lower_parts:
        packed = jnp.zeros((16, N), F32)
        for b in range(8):
            packed = jnp.where(group == b, part[16 * b : 16 * b + 16], packed)
        rows.append(packed)
    packed = jnp.concatenate(rows, axis=0)
    lane = iota((16 * count, N), 1)
    result = (lane % 16 == iota((16 * count, N), 0) % 16).astype(F32).reshape(count, 16, N)
    for j in range(15):
        factor = jnp.take_along_axis(packed, lane // 16 * 16 + j, axis=1).reshape(count, 16, N)
        result = result - factor * result[:, j : j + 1, :]
    return [
        jnp.concatenate([jnp.where(group == b, result[c], 0.0) for b in range(8)], axis=0)
        for c in range(count)
    ]


def merge(inverse, lower_part, size):
    starts = range(size, N, 2 * size)

    def pick(x):
        return jnp.concatenate([x[s : s + size] for s in starts], axis=0)

    half = (N // 2, N)
    row_pair = iota(half, 0) // size
    link = jnp.where(iota(half, 1) // size == 2 * row_pair, pick(lower_part), 0.0)
    hi, lo = split(inverse)
    linked = split(dot4(split(link), (hi, lo)))

    def spread(x):
        zero = jnp.zeros((size, N), BF16)
        pieces = []
        for p in range(len(starts)):
            pieces += [zero, x[p * size : (p + 1) * size]]
        return jnp.concatenate(pieces, axis=0)

    picked = pick(inverse)
    new = picked - dot4((pick(hi), pick(lo)), (spread(linked[0]), spread(linked[1])))
    pieces = []
    for p, s in enumerate(starts):
        pieces += [inverse[s - size : s], new[p * size : (p + 1) * size]]
    return jnp.concatenate(pieces, axis=0)


def blocks_kernel(x_ref, wu_ref, ph_ref, aux_ref, pair_ref, state):
    step = pl.program_id(0)
    eye = iota((N, N), 0) == iota((N, N), 1)
    strict = iota((N, N), 0) > iota((N, N), 1)

    @pl.when(step == 0)
    def _():
        start = (iota((N, 2 * N), 0) == iota((N, 2 * N), 1)).astype(F32)
        for h in range(HEADS):
            state[h] = start

    lower_parts, scales, keys = [], [], []
    for b in range(STEP):
        gates = x_ref[b, G0 : G0 + 16]
        cumulative_row = gate_rows(gates)
        cumulative_col, beta_col = gate_columns(gates)
        beta_row = gates.astype(F32)
        norm_rows = []
        for kh in range(KEYS):
            key = x_ref[b, kh * N : (kh + 1) * N]
            gram = dot_nt(key, key)
            diagonal = jnp.where(eye, gram, 0.0)
            norm_row = lax.rsqrt(jnp.sum(diagonal, axis=0, keepdims=True) + 1e-06)
            norm_col = lax.rsqrt(jnp.sum(diagonal, axis=1, keepdims=True) + 1e-06)
            norm_rows.append(norm_row)
            gram = jnp.where(strict, gram * norm_col * norm_row, 0.0)
            for h in range(2 * kh, 2 * kh + 2):
                crow = cumulative_row[4 + h : 5 + h]
                ccol = cumulative_col[:, 4 + h : 5 + h]
                decay = jnp.exp(jnp.minimum(ccol - crow, 0.0))
                lower_parts.append(gram * decay * beta_col[:, h : h + 1])
                last = crow[:, N - 1 : N]
                brow = beta_row[h : h + 1]
                scales.append((
                    brow * jnp.exp(crow) * norm_row,
                    brow,
                    norm_col * jnp.exp(last - ccol),
                    jnp.exp(last),
                ))
                keys.append((b, kh, h))
        aux_ref[b] = jnp.concatenate([cumulative_row[4:8]] + norm_rows + [jnp.zeros((2, N), F32)], axis=0)
    inverses = small_inverses(lower_parts)
    for size in (16, 32, 64):
        inverses = [merge(t, g, size) for t, g in zip(inverses, lower_parts)]
    transitions = []
    for inverse, (for_w, for_u, for_state, last), (b, kh, h) in zip(inverses, scales, keys):
        key = x_ref[b, kh * N : (kh + 1) * N]
        value = x_ref[b, V0 + h * N : V0 + (h + 1) * N]
        w = dot(jnp.concatenate(split(inverse * for_w), axis=1), jnp.concatenate([key, key], axis=0))
        u = dot(jnp.concatenate(split(inverse * for_u), axis=1), jnp.concatenate([value, value], axis=0))
        wu = jnp.concatenate([w, u], axis=1)
        wu_ref[b, h] = wu
        ab = dot_tn(
            jnp.concatenate([key, key], axis=0), jnp.concatenate(split(wu * for_state), axis=0)
        )
        transitions.append((
            left(split(jnp.where(eye, last, 0.0) - ab[:, :N])),
            ab[:, N:],
        ))
    for (a, offset), (b, kh, h) in zip(transitions, keys):
        hi, lo = split(state[h])
        ph_ref[b, h] = jnp.concatenate([hi, lo], axis=0)
        moved = dot(a, right((hi, lo)))
        state[h, :, :N] = moved[:, :N]
        state[h, :, N:] = moved[:, N:] + offset

    @pl.when(step == pl.num_programs(0) - 1)
    def _():
        for h in range(HEADS):
            pair_ref[h, :N] = state[h, :, :N].T
            pair_ref[h, N:] = state[h, :, N:].T


def blocks(x):
    steps = BLOCKS // STEP
    return pl.pallas_call(
        blocks_kernel,
        grid=(steps,),
        in_specs=[pl.BlockSpec((STEP, ROWS, N), lambda i: (i, 0, 0))],
        out_specs=[
            pl.BlockSpec((STEP, HEADS, N, 2 * N), lambda i: (i, 0, 0, 0)),
            pl.BlockSpec((STEP, HEADS, 2 * N, 2 * N), lambda i: (i, 0, 0, 0)),
            pl.BlockSpec((STEP, 8, N), lambda i: (i, 0, 0)),
            pl.BlockSpec((HEADS, 2 * N, N), lambda i: (0, 0, 0)),
        ],
        out_shape=[
            jax.ShapeDtypeStruct((BLOCKS, HEADS, N, 2 * N), F32),
            jax.ShapeDtypeStruct((BLOCKS, HEADS, 2 * N, 2 * N), BF16),
            jax.ShapeDtypeStruct((BLOCKS, 8, N), F32),
            jax.ShapeDtypeStruct((HEADS, 2 * N, N), F32),
        ],
        scratch_shapes=[pltpu.VMEM((HEADS, N, 2 * N), F32)],
        compiler_params=pltpu.CompilerParams(
            dimension_semantics=("arbitrary",), vmem_limit_bytes=48 * 2**20
        ),
        cost_estimate=pl.CostEstimate(flops=10**9, bytes_accessed=10 * 2**20, transcendentals=10**6),
        name="blocks",
    )(x)


def rows_kernel(x_ref, wu_ref, ph_ref, aux_ref, r_ref, o_ref):
    inclusive = iota((N, N), 0) >= iota((N, N), 1)
    gates = x_ref[0, G0 : G0 + 16]
    cumulative_col, _ = gate_columns(gates)
    for kh in range(KEYS):
        key = x_ref[0, kh * N : (kh + 1) * N]
        query = x_ref[0, Q0 + kh * N : Q0 + (kh + 1) * N]
        wide = query.astype(F32)
        norm = lax.rsqrt(jnp.sum(wide * wide, axis=1, keepdims=True) + 1e-06) * N ** (-0.5)
        unit = wide * norm
        scores = dot_nt(query, key) * norm * aux_ref[0, 4 + kh : 5 + kh]
        scores = jnp.where(inclusive, scores, 0.0)
        for h in range(2 * kh, 2 * kh + 2):
            ccol = cumulative_col[:, 4 + h : 5 + h]
            decay = jnp.exp(jnp.minimum(ccol - aux_ref[0, h : h + 1], 0.0))
            inner = dot4(split(scores * decay), split(wu_ref[0, h]))
            reach = split(unit * jnp.exp(ccol) - inner[:, :N])
            ph = ph_ref[0, h]
            both = dot(left(reach), right((ph[:N], ph[N:])))
            r_ref[0, h] = jnp.concatenate(split(both[:, :N]), axis=1)
            o_ref[0, h] = both[:, N:] + inner[:, N:]


def rows(x, wu, ph, aux):
    def spec(*shape):
        return pl.BlockSpec((1,) + shape, lambda i: (i,) + (0,) * len(shape))

    return pl.pallas_call(
        rows_kernel,
        grid=(BLOCKS,),
        in_specs=[spec(ROWS, N), spec(HEADS, N, 2 * N), spec(HEADS, 2 * N, 2 * N), spec(8, N)],
        out_specs=[spec(HEADS, N, 2 * N), spec(HEADS, N, N)],
        out_shape=[
            jax.ShapeDtypeStruct((BLOCKS, HEADS, N, 2 * N), BF16),
            jax.ShapeDtypeStruct((BLOCKS, HEADS, N, N), F32),
        ],
        compiler_params=pltpu.CompilerParams(
            dimension_semantics=("arbitrary",), vmem_limit_bytes=32 * 2**20
        ),
        cost_estimate=pl.CostEstimate(flops=2 * 10**9, bytes_accessed=14 * 2**20, transcendentals=10**6),
        name="rows",
    )(x, wu, ph, aux)


def prefix_kernel(pairs_ref, prefix_ref, total_ref):
    width = N + N // 2
    prefix_ref[0] = jnp.where(iota((width, N), 0) == iota((width, N), 1), 1.0, 0.0)
    running = pairs_ref[0]
    for s in range(1, 8):
        prefix_ref[s] = running
        nxt = pairs_ref[s]
        running = dot4(split(running), split(nxt[:N]))
        running = running + jnp.concatenate([jnp.zeros((N, N), F32), nxt[N:]], axis=0)
    total_ref[...] = running


def prefix(pairs):
    width = N + N // 2
    return pl.pallas_call(
        prefix_kernel,
        out_shape=[
            jax.ShapeDtypeStruct((8, width, N), F32),
            jax.ShapeDtypeStruct((width, N), F32),
        ],
        name="prefix",
    )(pairs)


def incoming_kernel(group_ref, prefix_ref, g1_ref, g2_ref, g3_ref, out_ref):
    group = group_ref[0]
    others = (g1_ref, g2_ref, g3_ref)
    state = jnp.zeros((N // 2, N), F32)
    for back in (3, 2, 1):
        other = others[back - 1]
        moved = dot4(split(state), split(other[:N])) + other[N:]
        state = jnp.where(back <= group, moved, state)
    state = left(split(state))
    for s in range(8):
        out_ref[s] = dot(state, right(split(prefix_ref[s, :N]))) + prefix_ref[s, N:]


def incoming(group, prefixes, others):
    vmem = pl.BlockSpec(memory_space=pltpu.VMEM)
    return pl.pallas_call(
        incoming_kernel,
        in_specs=[pl.BlockSpec(memory_space=pltpu.SMEM)] + [vmem] * 4,
        out_shape=jax.ShapeDtypeStruct((8, N // 2, N), F32),
        name="incoming",
    )(group, prefixes, *others)


def finish_kernel(r_ref, o_ref, s_ref, out_ref, state):
    @pl.when(pl.program_id(0) == 0)
    def _():
        for h in range(HEADS):
            hi, lo = split(s_ref[h])
            state[h] = jnp.concatenate([hi, hi, lo, lo], axis=1)

    for h in range(HEADS):
        r = r_ref[0, h]
        out = dot_nt(jnp.concatenate([r, r], axis=1), state[h]) + o_ref[0, h]
        out_ref[0, h] = out.astype(BF16)


def finish(r, o, s):
    def spec(*shape):
        return pl.BlockSpec((1,) + shape, lambda i: (i,) + (0,) * len(shape))

    return pl.pallas_call(
        finish_kernel,
        grid=(BLOCKS,),
        in_specs=[
            spec(HEADS, N, 2 * N),
            spec(HEADS, N, N),
            pl.BlockSpec((HEADS, N, N), lambda i: (0, 0, 0)),
        ],
        out_specs=spec(HEADS, N, N),
        out_shape=jax.ShapeDtypeStruct((BLOCKS, HEADS, N, N), BF16),
        scratch_shapes=[pltpu.VMEM((HEADS, N, 4 * N), BF16)],
        compiler_params=pltpu.CompilerParams(dimension_semantics=("arbitrary",)),
        name="finish",
    )(r, o, s)


def pack(query_rows, key_rows, value_rows, beta_rows, log_gate):
    def by_owner(x):
        owned = x.reshape(N, 8, -1, N).transpose(1, 2, 0, 3)
        return owned.reshape(8, -1, N)

    def gates(x):
        return x.T.reshape(8, HEADS, N)

    fill = jnp.zeros((8, ROWS - G0 - 2 * HEADS, N), BF16)
    return jnp.concatenate(
        [
            by_owner(key_rows),
            by_owner(query_rows),
            by_owner(value_rows),
            gates(beta_rows),
            gates(log_gate),
            fill,
        ],
        axis=1,
    )


EIGHTS = [list(range(8 * g, 8 * g + 8)) for g in range(4)]


def states_before(pair):
    half = N // 2
    a = jnp.broadcast_to(pair[:, None, :N], (HEADS, 2, N, N))
    b = pair[:, N:].reshape(HEADS, 2, half, N)
    send = jnp.concatenate([a, b], axis=2).reshape(8, N + half, N)
    got = lax.all_to_all(send, "ctx", 0, 0, tiled=True, axis_index_groups=EIGHTS)
    prefixes, total = prefix(got)
    others = []
    for back in (1, 2, 3):
        ring = [(i, (i + 8 * back) % 32) for i in range(32)]
        others.append(lax.ppermute(total, "ctx", ring))
    group = (lax.axis_index("ctx") // 8).astype(jnp.int32).reshape(1)
    states = incoming(group, prefixes, others)
    mine = lax.all_to_all(states, "ctx", 0, 0, tiled=True, axis_index_groups=EIGHTS)
    return mine.reshape(HEADS, N, N)


def local(query_rows, key_rows, value_rows, beta_rows, log_gate):
    packed = pack(query_rows, key_rows, value_rows, beta_rows, log_gate)
    x = lax.all_to_all(packed, "head", 0, 0, tiled=True)
    wu, ph, aux, pair = blocks(x)
    state = states_before(pair)
    r, o = rows(x, wu, ph, aux)
    out = finish(r, o, state)
    back = lax.all_to_all(out, "head", 0, 0, tiled=True)
    return back.reshape(8 * HEADS, N, N).transpose(1, 0, 2)


def solution(mesh):
    placed = (
        P(("ctx", "head"), None, None),
        P(("ctx", "head"), None, None),
        P(("ctx", "head"), None, None),
        P(("ctx", "head"), None),
        P(("ctx", "head"), None),
    )
    return jax.shard_map(
        local, mesh=mesh, in_specs=placed, out_specs=P(("ctx", "head"), None, None), check_vma=False
    )
```

```python
import functools

import jax
import jax.numpy as jnp
from jax import lax
from jax.experimental import pallas as pl
from jax.experimental.pallas import tpu as pltpu
from jax.sharding import PartitionSpec as P

N = 128
CHIPS = 16
SPANS = 4
PAIRS = 4
Q0, G0 = N, 2 * N
KROWS = 2 * N + 16
F32, BF16 = jnp.float32, jnp.bfloat16


def iota(shape, dim):
    return lax.broadcasted_iota(jnp.int32, shape, dim)


def split(x):
    hi = x.astype(BF16)
    return hi, (x - hi.astype(F32)).astype(BF16)


def dot(a, b):
    return jnp.dot(a, b, preferred_element_type=F32)


def dot_nt(a, b):
    return lax.dot_general(a, b, (((1,), (1,)), ((), ())), preferred_element_type=F32)


def dot_tn(a, b):
    return lax.dot_general(a, b, (((0,), (0,)), ((), ())), preferred_element_type=F32)


def dot3(a, b):
    return dot(a[0], b[0]) + dot(a[0], b[1]) + dot(a[1], b[0])


def dot4(a, b):
    wide = jnp.concatenate([a[0], a[1], a[0], a[1]], axis=1)
    return dot(wide, jnp.concatenate([b[0], b[0], b[1], b[1]], axis=0))


def halves(x):
    return x[:, :N], x[:, N:]


def gate_rows(gates):
    upper = (iota((N, N), 0) <= iota((N, N), 1)).astype(F32).astype(BF16)
    return dot(gates, upper)


def gate_columns(gates):
    lower = (iota((N, N), 0) >= iota((N, N), 1)).astype(F32).astype(BF16)
    eye = (iota((N, N), 0) == iota((N, N), 1)).astype(F32).astype(BF16)
    both = dot_nt(jnp.concatenate([lower, eye], axis=0), gates)
    return both[:N], both[N:]


def small_inverses(lower_parts):
    count = len(lower_parts)
    group = iota((16, N), 1) // 16
    rows = []
    for part in lower_parts:
        packed = jnp.zeros((16, N), F32)
        for b in range(8):
            packed = jnp.where(group == b, part[16 * b : 16 * b + 16], packed)
        rows.append(packed)
    packed = jnp.concatenate(rows, axis=0)
    lane = iota((16 * count, N), 1)
    result = (lane % 16 == iota((16 * count, N), 0) % 16).astype(F32).reshape(count, 16, N)
    for j in range(15):
        factor = jnp.take_along_axis(packed, lane // 16 * 16 + j, axis=1).reshape(count, 16, N)
        result = result - factor * result[:, j : j + 1, :]
    return [
        jnp.concatenate([jnp.where(group == b, result[c], 0.0) for b in range(8)], axis=0)
        for c in range(count)
    ]


def merge(inverse, lower_part, size):
    starts = range(size, N, 2 * size)

    def pick(x):
        return jnp.concatenate([x[s : s + size] for s in starts], axis=0)

    half = (N // 2, N)
    row_pair = iota(half, 0) // size
    link = jnp.where(iota(half, 1) // size == 2 * row_pair, pick(lower_part), 0.0)
    hi, lo = split(inverse)
    linked = split(dot3(split(link), (hi, lo)))

    def spread(x):
        zero = jnp.zeros((size, N), BF16)
        pieces = []
        for p in range(len(starts)):
            pieces += [zero, x[p * size : (p + 1) * size]]
        return jnp.concatenate(pieces, axis=0)

    picked = pick(inverse)
    new = picked - dot3((pick(hi), pick(lo)), (spread(linked[0]), spread(linked[1])))
    pieces = []
    for p, s in enumerate(starts):
        pieces += [inverse[s - size : s], new[p * size : (p + 1) * size]]
    return jnp.concatenate(pieces, axis=0)


def params(megabytes):
    return pltpu.CompilerParams(
        dimension_semantics=("arbitrary",), vmem_limit_bytes=megabytes * 2**20
    )


def cost(flops, megabytes):
    return pl.CostEstimate(flops=flops, bytes_accessed=megabytes * 2**20, transcendentals=10**6)


def in_hbm(*arrays):
    return [pltpu.with_memory_space_constraint(x, pltpu.HBM) for x in arrays]


def core_here():
    return lax.axis_index("head") % 2


def group_here():
    return lax.axis_index("ctx") // 4


def spec(*shape):
    return pl.BlockSpec(shape, lambda i: (i,) + (0,) * (len(shape) - 1))


STEP = 4


def solve_kernel(x0_ref, x1_ref, aux_ref, w_ref, tu_ref, m_ref, a_ref):
    first = core_here() == 0
    units = [(x_ref, b, which) for which, x_ref in enumerate((x0_ref, x1_ref)) for b in range(STEP)]
    eye = iota((N, N), 0) == iota((N, N), 1)
    strict = iota((N, N), 0) > iota((N, N), 1)
    lower_parts, scales = [], []
    for x_ref, b, which in units:
        key = x_ref[b, :N]
        gates = x_ref[b, G0 : G0 + 16]
        rows_here = gate_rows(gates)
        cols_here, beta_cols = gate_columns(gates)
        wide = gates.astype(F32)
        brow = jnp.where(first, wide[0:1], wide[1:2])
        bcol = jnp.where(first, beta_cols[:, 0:1], beta_cols[:, 1:2])
        crow = jnp.where(first, rows_here[2:3], rows_here[3:4])
        ccol = jnp.where(first, cols_here[:, 2:3], cols_here[:, 3:4])
        gram = dot_nt(key, key)
        diagonal = jnp.where(eye, gram, 0.0)
        norm_row = lax.rsqrt(jnp.sum(diagonal, axis=0, keepdims=True) + 1e-06)
        norm_col = lax.rsqrt(jnp.sum(diagonal, axis=1, keepdims=True) + 1e-06)
        decay = jnp.exp(jnp.minimum(ccol - crow, 0.0))
        scaled = gram * (norm_col * bcol) * norm_row * decay
        lower_parts.append(jnp.where(strict, scaled, 0.0))
        last = crow[:, N - 1 : N]
        scales.append((
            brow * jnp.exp(crow) * norm_row,
            brow,
            norm_col * jnp.exp(last - ccol),
            jnp.exp(last),
        ))
        aux_ref[b, which] = jnp.concatenate([crow, norm_row, jnp.zeros((6, N), F32)], axis=0)
    inverses = small_inverses(lower_parts)
    for size in (16, 32, 64):
        inverses = [merge(t, g, size) for t, g in zip(inverses, lower_parts)]
    for inverse, (for_w, for_u, for_state, last), (x_ref, b, which) in zip(inverses, scales, units):
        key = x_ref[b, :N]
        hi, lo = split(inverse * for_w)
        w = dot(hi, key) + dot(lo, key)
        tu = inverse * for_u
        tu_ref[b, which] = jnp.concatenate(split(tu), axis=1)
        w_ref[b, which] = w
        hi, lo = split(jnp.concatenate([w, tu], axis=1) * for_state)
        both = dot_tn(key, hi) + dot_tn(key, lo)
        a_ref[b, which] = jnp.concatenate(split(jnp.where(eye, last, 0.0) - both[:, :N]), axis=1)
        m_ref[b, which] = jnp.concatenate(split(both[:, N:]), axis=1)


def solve(x0, x1):
    return pl.pallas_call(
        solve_kernel,
        grid=(CHIPS // STEP,),
        in_specs=[spec(STEP, KROWS, N)] * 2,
        out_specs=[spec(STEP, 2, 8, N), spec(STEP, 2, N, N)] + [spec(STEP, 2, N, 2 * N)] * 3,
        out_shape=[
            pltpu.HBM((CHIPS, 2, 8, N), F32),
            pltpu.HBM((CHIPS, 2, N, N), F32),
        ]
        + [pltpu.HBM((CHIPS, 2, N, 2 * N), BF16)] * 3,
        compiler_params=params(24),
        cost_estimate=cost(16 * 10**9, 20),
        name="solve",
    )(x0, x1)


def later(a, offset, parts):
    moved = dot4(a, parts)
    return jnp.concatenate([moved[:, :N], moved[:, N:] + offset], axis=1)


def unit_pair():
    return jnp.where(iota((N, 2 * N), 0) == iota((N, 2 * N), 1), 1.0, 0.0)


def chain_kernel(m_ref, a_ref, v_ref, ph_ref, start_ref, total_ref, state):
    step = pl.program_id(0)

    @pl.when(step == 0)
    def _():
        for s in range(SPANS):
            state[s] = unit_pair()

    def advance(order):
        for place, which in enumerate(order):
            for s in range(SPANS):
                value = v_ref[s, 0, place]
                hi, lo = halves(m_ref[s, 0, which])
                offset = dot(hi, value) + dot(lo, value)
                parts = split(state[s])
                ph_ref[s, 0, which] = jnp.concatenate(parts, axis=0)
                state[s] = later(halves(a_ref[s, 0, which]), offset, parts)

    @pl.when(core_here() == 0)
    def _():
        advance((0, 1))

    @pl.when(core_here() != 0)
    def _():
        advance((1, 0))

    @pl.when(step == PAIRS - 1)
    def _():
        running = state[0]
        start_ref[0] = unit_pair()
        for s in range(1, SPANS):
            start_ref[s] = running
            running = later(split(state[s, :, :N]), state[s, :, N:], split(running))
        total_ref[...] = running


def chain(m, a, v):
    def of_pair(*shape):
        return pl.BlockSpec((SPANS, 1) + shape, lambda i: (0, i) + (0,) * len(shape))

    m, a = (x.reshape(SPANS, PAIRS, 2, N, 2 * N) for x in (m, a))
    return pl.pallas_call(
        chain_kernel,
        grid=(PAIRS,),
        in_specs=[of_pair(2, N, 2 * N)] * 2 + [of_pair(2, N, N)],
        out_specs=[
            of_pair(2, 2 * N, 2 * N),
            pl.BlockSpec((SPANS, N, 2 * N), lambda i: (0, 0, 0)),
            pl.BlockSpec((N, 2 * N), lambda i: (0, 0)),
        ],
        out_shape=[
            jax.ShapeDtypeStruct((SPANS, PAIRS, 2, 2 * N, 2 * N), BF16),
            jax.ShapeDtypeStruct((SPANS, N, 2 * N), F32),
            jax.ShapeDtypeStruct((N, 2 * N), F32),
        ],
        scratch_shapes=[pltpu.VMEM((SPANS, N, 2 * N), F32)],
        compiler_params=params(16),
        cost_estimate=cost(4 * 10**9, 10),
        name="chain",
    )(*in_hbm(m, a), v.reshape(SPANS, PAIRS, 2, N, N))


ROWSTEP = 4


def rows_kernel(which, x_ref, v_ref, aux_ref, w_ref, tu_ref, ph_ref, r_ref, o_ref):
    core = core_here()
    first = core == 0
    place = core if which == 0 else 1 - core
    inclusive = iota((N, N), 0) >= iota((N, N), 1)
    for b in range(ROWSTEP):
        key, query, value = x_ref[b, :N], x_ref[b, Q0 : Q0 + N], v_ref[b, place]
        cols_here, _ = gate_columns(x_ref[b, G0 : G0 + 16])
        ccol = jnp.where(first, cols_here[:, 2:3], cols_here[:, 3:4])
        wide = query.astype(F32)
        norm = lax.rsqrt(jnp.sum(wide * wide, axis=1, keepdims=True) + 1e-06) * N ** (-0.5)
        decay = jnp.exp(jnp.minimum(ccol - aux_ref[b, 0:1], 0.0))
        scores = dot_nt(query, key) * norm * aux_ref[b, 1:2] * decay
        scores = jnp.where(inclusive, scores, 0.0)
        hi, lo = halves(tu_ref[b])
        u = dot(hi, value) + dot(lo, value)
        inner = dot4(split(scores), split(jnp.concatenate([w_ref[b], u], axis=1)))
        reach = split(wide * (norm * jnp.exp(ccol)) - inner[:, :N])
        both = dot4(reach, (ph_ref[b, :N], ph_ref[b, N:]))
        r_ref[b] = jnp.concatenate(split(both[:, :N]), axis=1)
        o_ref[b] = both[:, N:] + inner[:, N:]


def rows(which, x, v, aux, w, tu, ph):
    def one_of(*shape):
        return pl.BlockSpec((ROWSTEP, None) + shape, lambda i: (i, which) + (0,) * len(shape))

    return pl.pallas_call(
        functools.partial(rows_kernel, which),
        grid=(CHIPS // ROWSTEP,),
        in_specs=[
            spec(ROWSTEP, KROWS, N),
            spec(ROWSTEP, 2, N, N),
            one_of(8, N),
            one_of(N, N),
            one_of(N, 2 * N),
            one_of(2 * N, 2 * N),
        ],
        out_specs=[spec(ROWSTEP, N, 2 * N), spec(ROWSTEP, N, N)],
        out_shape=[
            jax.ShapeDtypeStruct((CHIPS, N, 2 * N), BF16),
            jax.ShapeDtypeStruct((CHIPS, N, N), F32),
        ],
        compiler_params=params(16),
        cost_estimate=cost(5 * 10**9, 8),
        name="rows",
    )(x, v.reshape(CHIPS, 2, N, N), aux, w, tu, ph.reshape(CHIPS, 2, 2 * N, 2 * N))


def first_join_kernel(got_ref, own_ref, before_ref, run_ref):
    before = jnp.where(group_here() >= 1, got_ref[...], unit_pair())
    own = own_ref[...]
    before_ref[...] = before
    run_ref[...] = later(split(own[:, :N]), own[:, N:], split(before))


def second_join_kernel(got_ref, before_ref, run_ref, longer_ref, offset_ref):
    got = split(jnp.where(group_here() >= 2, got_ref[...], unit_pair()))
    run, before = run_ref[...], before_ref[...]
    offset_ref[...] = dot4(split(run[:, :N]), (got[0][:, N:], got[1][:, N:])) + run[:, N:]
    longer_ref[...] = later(split(before[:, :N]), before[:, N:], got)


def joined(kernel, outs, *args):
    vmem = pl.BlockSpec(memory_space=pltpu.VMEM)
    return pl.pallas_call(
        kernel,
        in_specs=[vmem] * len(args),
        out_shape=[jax.ShapeDtypeStruct((N, width), F32) for width in outs],
        compiler_params=pltpu.CompilerParams(vmem_limit_bytes=8 * 2**20),
    )(*args)


def finish_kernel(got_ref, longer_ref, start_ref, r0, o0, r1, o1, out_ref, state):
    step = pl.program_id(0)

    @pl.when(step == 0)
    def _():
        offset = jnp.where(group_here() >= 4, got_ref[...], 0.0)
        before = longer_ref[...]
        first = dot4(split(before[:, :N]), split(offset)) + before[:, N:]
        parts = split(first)
        state[0] = jnp.concatenate(parts, axis=0)
        for s in range(1, SPANS):
            pair = start_ref[s]
            state[s] = jnp.concatenate(
                split(dot4(split(pair[:, :N]), parts) + pair[:, N:]), axis=0
            )

    rhs = state[step]
    core = core_here()
    for b in range(PAIRS):
        for place, r_ref, o_ref in ((core, r0, o0), (1 - core, r1, o1)):
            out = dot4(halves(r_ref[b]), (rhs[:N], rhs[N:])) + o_ref[b]
            out_ref[b, place] = out.astype(BF16)


def finish(got, longer, start, r0, o0, r1, o1):
    return pl.pallas_call(
        finish_kernel,
        grid=(SPANS,),
        in_specs=[
            pl.BlockSpec((N, N), lambda i: (0, 0)),
            pl.BlockSpec((N, 2 * N), lambda i: (0, 0)),
            pl.BlockSpec((SPANS, N, 2 * N), lambda i: (0, 0, 0)),
        ]
        + [spec(PAIRS, N, 2 * N), spec(PAIRS, N, N)] * 2,
        out_specs=spec(PAIRS, 2, N, N),
        out_shape=jax.ShapeDtypeStruct((CHIPS, 2, N, N), BF16),
        scratch_shapes=[pltpu.VMEM((SPANS, 2 * N, N), BF16)],
        compiler_params=params(16),
        cost_estimate=cost(10**9, 5),
        name="finish",
    )(got, longer, start, r0, o0, r1, o1)


PACKSTEP = 32


def pack_kernel(k_ref, q_ref, beta_ref, gate_ref, out_ref, wide):
    step = pl.program_id(0)
    for start, ref in ((0, k_ref), (Q0, q_ref)):
        wide[start // N] = ref[...].astype(F32).reshape(16 * PACKSTEP, N)
        row = pl.multiple_of(start + step * PACKSTEP, PACKSTEP)
        for h in range(16):
            rows = wide[start // N, pl.ds(h, PACKSTEP, stride=16), :]
            out_ref[h, pl.ds(row, PACKSTEP), :] = rows.astype(BF16)

    @pl.when(step == 0)
    def _():
        beta, gate = beta_ref[...].astype(F32), gate_ref[...].astype(F32)
        for h in range(16):
            pair = slice(2 * h, 2 * h + 2)
            tail = jnp.concatenate([beta[pair], gate[pair], jnp.zeros((12, N), F32)], axis=0)
            out_ref[h, G0:] = tail.astype(BF16)


def pack(key_rows, query_rows, beta_rows, log_gate):
    return pl.pallas_call(
        pack_kernel,
        grid=(N // PACKSTEP,),
        in_specs=[spec(PACKSTEP, 16, N)] * 2 + [pl.BlockSpec((32, N), lambda i: (0, 0))] * 2,
        out_specs=pl.BlockSpec((CHIPS, KROWS, N), lambda i: (0, 0, 0)),
        out_shape=jax.ShapeDtypeStruct((CHIPS, KROWS, N), BF16),
        scratch_shapes=[pltpu.VMEM((2, 16 * PACKSTEP, N), F32)],
        compiler_params=params(60),
        name="pack",
    )(key_rows, query_rows, beta_rows.T, log_gate.T)


EVERY = [list(range(32 * g, 32 * g + 32)) for g in range(8)]
ALIKE = [list(range(32 * g + core, 32 * g + 32, 2)) for g in range(8) for core in range(2)]


def exchange(x, groups):
    return lax.all_to_all(x, ("ctx", "head"), 0, 0, tiled=True, axis_index_groups=groups)


def onward(x, groups):
    ring = [(i, (i + 4 * groups) % 32) for i in range(32)]
    return lax.ppermute(x, "ctx", ring)


def other_core(x):
    return lax.ppermute(x, "head", [(i, i ^ 1) for i in range(8)])


def local(query_rows, key_rows, value_rows, beta_rows, log_gate):
    x0 = exchange(pack(key_rows, query_rows, beta_rows, log_gate), ALIKE)
    values, x0 = lax.optimization_barrier((value_rows.transpose(1, 0, 2), x0))
    x1 = other_core(x0)
    v = exchange(values, EVERY)
    aux, w, tu, m, a = solve(x0, x1)
    ph, start, total = chain(m, a, v)
    before, run = joined(first_join_kernel, (2 * N, 2 * N), onward(total, 1), total)
    longer, offset = joined(second_join_kernel, (2 * N, N), onward(run, 2), before, run)
    got = onward(offset, 4)
    r0, o0 = rows(0, x0, v, aux, w, tu, ph)
    r1, o1 = rows(1, x1, v, aux, w, tu, ph)
    out = finish(got, longer, start, r0, o0, r1, o1)
    return exchange(out.reshape(2 * CHIPS, N, N), EVERY).transpose(1, 0, 2)


def solution(mesh):
    placed = (
        P(("ctx", "head"), None, None),
        P(("ctx", "head"), None, None),
        P(("ctx", "head"), None, None),
        P(("ctx", "head"), None),
        P(("ctx", "head"), None),
    )
    return jax.shard_map(
        local, mesh=mesh, in_specs=placed, out_specs=P(("ctx", "head"), None, None), check_vma=False
    )
```

```python
import functools

import jax
import jax.numpy as jnp
from jax import lax
from jax.experimental import pallas as pl
from jax.experimental.pallas import tpu as pltpu
from jax.sharding import PartitionSpec as P

N = 128
CHIPS = 16
SPANS = 4
PAIRS = 4
Q0, G0 = N, 2 * N
KROWS = 2 * N + 16
F32, BF16 = jnp.float32, jnp.bfloat16


def iota(shape, dim):
    return lax.broadcasted_iota(jnp.int32, shape, dim)


def split(x):
    hi = x.astype(BF16)
    return hi, (x - hi.astype(F32)).astype(BF16)


def dot(a, b):
    return jnp.dot(a, b, preferred_element_type=F32)


def dot_nt(a, b):
    return lax.dot_general(a, b, (((1,), (1,)), ((), ())), preferred_element_type=F32)


def dot_tn(a, b):
    return lax.dot_general(a, b, (((0,), (0,)), ((), ())), preferred_element_type=F32)


def dot_stacked(stacked, b):
    rows = stacked.shape[0] // 2
    both = dot(stacked, b)
    return both[:rows] + both[rows:]


def stack(parts):
    return jnp.concatenate(parts, axis=0)


def dot3(a, b):
    return dot_stacked(stack(a), b[0]) + dot(a[0], b[1])


def dot4(a, b):
    wide = jnp.concatenate([a[0], a[1], a[0], a[1]], axis=1)
    return dot(wide, jnp.concatenate([b[0], b[0], b[1], b[1]], axis=0))


def halves(x):
    return x[:, :N], x[:, N:]


def gate_rows(gates):
    upper = (iota((N, N), 0) <= iota((N, N), 1)).astype(F32).astype(BF16)
    return dot(gates, upper)


def gate_columns(gates):
    lower = (iota((N, N), 0) >= iota((N, N), 1)).astype(F32).astype(BF16)
    eye = (iota((N, N), 0) == iota((N, N), 1)).astype(F32).astype(BF16)
    both = dot_nt(jnp.concatenate([lower, eye], axis=0), gates)
    return both[:N], both[N:]


def small_inverses(lower_parts):
    count = len(lower_parts)
    group = iota((16, N), 1) // 16
    rows = []
    for part in lower_parts:
        packed = jnp.zeros((16, N), F32)
        for b in range(8):
            packed = jnp.where(group == b, part[16 * b : 16 * b + 16], packed)
        rows.append(packed)
    packed = jnp.concatenate(rows, axis=0)
    lane = iota((16 * count, N), 1)
    result = (lane % 16 == iota((16 * count, N), 0) % 16).astype(F32).reshape(count, 16, N)
    for j in range(15):
        factor = jnp.take_along_axis(packed, lane // 16 * 16 + j, axis=1).reshape(count, 16, N)
        result = result - factor * result[:, j : j + 1, :]
    return [
        jnp.concatenate([jnp.where(group == b, result[c], 0.0) for b in range(8)], axis=0)
        for c in range(count)
    ]


def merge(parts, lower_part, size):
    starts = range(size, N, 2 * size)

    def pick(x):
        return jnp.concatenate([x[s : s + size] for s in starts], axis=0)

    half = (N // 2, N)
    link = jnp.where(iota(half, 1) // size == 2 * (iota(half, 0) // size), pick(lower_part), 0.0)
    linked = split(dot3(split(link), parts[1:]))

    def spread(x):
        zero = jnp.zeros((size, N), BF16)
        pieces = []
        for p in range(len(starts)):
            pieces += [zero, x[p * size : (p + 1) * size]]
        return jnp.concatenate(pieces, axis=0)

    picked = [pick(x) for x in parts]
    new = picked[0] - dot3(picked[1:], (spread(linked[0]), spread(linked[1])))

    def renew(old, fresh):
        pieces = []
        for p, s in enumerate(starts):
            pieces += [old[s - size : s], fresh[p * size : (p + 1) * size]]
        return jnp.concatenate(pieces, axis=0)

    return [renew(old, fresh) for old, fresh in zip(parts, (new,) + split(new))]


def params(megabytes):
    return pltpu.CompilerParams(
        dimension_semantics=("arbitrary",), vmem_limit_bytes=megabytes * 2**20
    )


def cost(flops, megabytes):
    return pl.CostEstimate(flops=flops, bytes_accessed=megabytes * 2**20, transcendentals=10**6)


def in_hbm(*arrays):
    return [pltpu.with_memory_space_constraint(x, pltpu.HBM) for x in arrays]


def core_here():
    return lax.axis_index("head") % 2


def group_here():
    return lax.axis_index("ctx") // 4


def spec(*shape):
    return pl.BlockSpec(shape, lambda i: (i,) + (0,) * (len(shape) - 1))


STEP = 16


def solve_kernel(x0_ref, x1_ref, aux_ref, w_ref, tu_ref, m_ref, a_ref):
    first = core_here() == 0
    units = [(x_ref, b, which) for which, x_ref in enumerate((x0_ref, x1_ref)) for b in range(STEP)]
    eye = iota((N, N), 0) == iota((N, N), 1)
    strict = iota((N, N), 0) > iota((N, N), 1)
    lower_parts, scales = [], []
    for x_ref, b, which in units:
        key = x_ref[b, :N]
        gates = x_ref[b, G0 : G0 + 16]
        rows_here = gate_rows(gates)
        cols_here, beta_cols = gate_columns(gates)
        wide = gates.astype(F32)
        brow = jnp.where(first, wide[0:1], wide[1:2])
        bcol = jnp.where(first, beta_cols[:, 0:1], beta_cols[:, 1:2])
        crow = jnp.where(first, rows_here[2:3], rows_here[3:4])
        ccol = jnp.where(first, cols_here[:, 2:3], cols_here[:, 3:4])
        gram = dot_nt(key, key)
        diagonal = jnp.where(eye, gram, 0.0)
        norm_row = lax.rsqrt(jnp.sum(diagonal, axis=0, keepdims=True) + 1e-06)
        norm_col = lax.rsqrt(jnp.sum(diagonal, axis=1, keepdims=True) + 1e-06)
        decay = jnp.exp(jnp.minimum(ccol - crow, 0.0))
        scaled = gram * (norm_col * bcol) * norm_row * decay
        lower_parts.append(jnp.where(strict, scaled, 0.0))
        last = crow[:, N - 1 : N]
        scales.append((
            brow * jnp.exp(crow) * norm_row,
            brow,
            norm_col * jnp.exp(last - ccol),
            jnp.exp(last),
        ))
        aux_ref[b, which] = jnp.concatenate([crow, norm_row, jnp.zeros((6, N), F32)], axis=0)
    inverses = [(t,) + split(t) for t in small_inverses(lower_parts)]
    for size in (16, 32, 64):
        inverses = [merge(t, g, size) for t, g in zip(inverses, lower_parts)]
    inverses = [t[0] for t in inverses]
    for inverse, (for_w, for_u, for_state, last), (x_ref, b, which) in zip(inverses, scales, units):
        key = x_ref[b, :N]
        w = dot_stacked(stack(split(inverse * for_w)), key)
        tu = inverse * for_u
        tu_ref[b, which] = stack(split(tu))
        w_ref[b, which] = w
        hi, lo = split(jnp.concatenate([w, tu], axis=1) * for_state)
        both = dot_tn(key, hi) + dot_tn(key, lo)
        a_ref[b, which] = jnp.concatenate(split(jnp.where(eye, last, 0.0) - both[:, :N]), axis=1)
        m_ref[b, which] = stack(split(both[:, N:]))


def solve(x0, x1):
    return pl.pallas_call(
        solve_kernel,
        grid=(CHIPS // STEP,),
        in_specs=[spec(STEP, KROWS, N)] * 2,
        out_specs=[spec(STEP, 2, 8, N), spec(STEP, 2, N, N)] + [spec(STEP, 2, 2 * N, N)] * 2 + [spec(STEP, 2, N, 2 * N)],
        out_shape=[
            pltpu.HBM((CHIPS, 2, 8, N), F32),
            pltpu.HBM((CHIPS, 2, N, N), F32),
        ]
        + [pltpu.HBM((CHIPS, 2, 2 * N, N), BF16)] * 2
        + [pltpu.HBM((CHIPS, 2, N, 2 * N), BF16)],
        compiler_params=params(24),
        cost_estimate=cost(16 * 10**9, 20),
        name="solve",
    )(x0, x1)


def later(a, offset, parts):
    moved = dot4(a, parts)
    return jnp.concatenate([moved[:, :N], moved[:, N:] + offset], axis=1)


def unit_pair():
    return jnp.where(iota((N, 2 * N), 0) == iota((N, 2 * N), 1), 1.0, 0.0)


def chain_kernel(m_ref, a_ref, v_ref, ph_ref, start_ref, total_ref, state):
    step = pl.program_id(0)

    @pl.when(step == 0)
    def _():
        for s in range(SPANS):
            state[s] = unit_pair()

    def advance(order):
        for place, which in enumerate(order):
            for s in range(SPANS):
                value = v_ref[s, 0, place]
                offset = dot_stacked(m_ref[s, 0, which], value)
                parts = split(state[s])
                ph_ref[s, 0, which] = jnp.concatenate(parts, axis=0)
                state[s] = later(halves(a_ref[s, 0, which]), offset, parts)

    @pl.when(core_here() == 0)
    def _():
        advance((0, 1))

    @pl.when(core_here() != 0)
    def _():
        advance((1, 0))

    @pl.when(step == PAIRS - 1)
    def _():
        running = state[0]
        start_ref[0] = unit_pair()
        for s in range(1, SPANS):
            start_ref[s] = running
            running = later(split(state[s, :, :N]), state[s, :, N:], split(running))
        total_ref[...] = running


def chain(m, a, v):
    def of_pair(*shape):
        return pl.BlockSpec((SPANS, 1) + shape, lambda i: (0, i) + (0,) * len(shape))

    m, a = m.reshape(SPANS, PAIRS, 2, 2 * N, N), a.reshape(SPANS, PAIRS, 2, N, 2 * N)
    return pl.pallas_call(
        chain_kernel,
        grid=(PAIRS,),
        in_specs=[of_pair(2, 2 * N, N), of_pair(2, N, 2 * N), of_pair(2, N, N)],
        out_specs=[
            of_pair(2, 2 * N, 2 * N),
            pl.BlockSpec((SPANS, N, 2 * N), lambda i: (0, 0, 0)),
            pl.BlockSpec((N, 2 * N), lambda i: (0, 0)),
        ],
        out_shape=[
            jax.ShapeDtypeStruct((SPANS, PAIRS, 2, 2 * N, 2 * N), BF16),
            jax.ShapeDtypeStruct((SPANS, N, 2 * N), F32),
            jax.ShapeDtypeStruct((N, 2 * N), F32),
        ],
        scratch_shapes=[pltpu.VMEM((SPANS, N, 2 * N), F32)],
        compiler_params=params(16),
        cost_estimate=cost(4 * 10**9, 10),
        name="chain",
    )(*in_hbm(m, a), v.reshape(SPANS, PAIRS, 2, N, N))


ROWSTEP = 8


def rows_kernel(which, x_ref, v_ref, aux_ref, w_ref, tu_ref, ph_ref, r_ref, o_ref):
    core = core_here()
    first = core == 0
    place = core if which == 0 else 1 - core
    inclusive = iota((N, N), 0) >= iota((N, N), 1)
    for b in range(ROWSTEP):
        key, query, value = x_ref[b, :N], x_ref[b, Q0 : Q0 + N], v_ref[b, place]
        cols_here, _ = gate_columns(x_ref[b, G0 : G0 + 16])
        ccol = jnp.where(first, cols_here[:, 2:3], cols_here[:, 3:4])
        wide = query.astype(F32)
        norm = lax.rsqrt(jnp.sum(wide * wide, axis=1, keepdims=True) + 1e-06) * N ** (-0.5)
        decay = jnp.exp(jnp.minimum(ccol - aux_ref[b, 0:1], 0.0))
        scores = dot_nt(query, key) * norm * aux_ref[b, 1:2] * decay
        scores = jnp.where(inclusive, scores, 0.0)
        u = dot_stacked(tu_ref[b], value)
        inner = dot4(split(scores), split(jnp.concatenate([w_ref[b], u], axis=1)))
        reach = split(wide * (norm * jnp.exp(ccol)) - inner[:, :N])
        both = dot4(reach, (ph_ref[b, :N], ph_ref[b, N:]))
        r_ref[b] = jnp.concatenate(split(both[:, :N]), axis=1)
        o_ref[b] = both[:, N:] + inner[:, N:]


def rows(which, first, count, x, v, aux, w, tu, ph):
    def at(i):
        return first // ROWSTEP + i

    def some(*shape):
        return pl.BlockSpec((ROWSTEP,) + shape, lambda i: (at(i),) + (0,) * len(shape))

    def one_of(*shape):
        return pl.BlockSpec((ROWSTEP, None) + shape, lambda i: (at(i), which) + (0,) * len(shape))

    return pl.pallas_call(
        functools.partial(rows_kernel, which),
        grid=(count // ROWSTEP,),
        in_specs=[
            some(KROWS, N),
            some(2, N, N),
            one_of(8, N),
            one_of(N, N),
            one_of(2 * N, N),
            one_of(2 * N, 2 * N),
        ],
        out_specs=[spec(ROWSTEP, N, 2 * N), spec(ROWSTEP, N, N)],
        out_shape=[
            jax.ShapeDtypeStruct((count, N, 2 * N), BF16),
            jax.ShapeDtypeStruct((count, N, N), F32),
        ],
        compiler_params=params(20),
        cost_estimate=cost(count * 3 * 10**8, count // 2),
        name="rows",
    )(x, v.reshape(CHIPS, 2, N, N), aux, w, tu, ph.reshape(CHIPS, 2, 2 * N, 2 * N))


def first_join_kernel(got_ref, own_ref, before_ref, run_ref):
    before = jnp.where(group_here() >= 1, got_ref[...], unit_pair())
    own = own_ref[...]
    before_ref[...] = before
    run_ref[...] = later(split(own[:, :N]), own[:, N:], split(before))


def second_join_kernel(got_ref, before_ref, run_ref, longer_ref, offset_ref):
    got = split(jnp.where(group_here() >= 2, got_ref[...], unit_pair()))
    run, before = run_ref[...], before_ref[...]
    offset_ref[...] = dot4(split(run[:, :N]), (got[0][:, N:], got[1][:, N:])) + run[:, N:]
    longer_ref[...] = later(split(before[:, :N]), before[:, N:], got)


def joined(kernel, outs, *args):
    vmem = pl.BlockSpec(memory_space=pltpu.VMEM)
    return pl.pallas_call(
        kernel,
        in_specs=[vmem] * len(args),
        out_shape=[jax.ShapeDtypeStruct((N, width), F32) for width in outs],
        compiler_params=pltpu.CompilerParams(vmem_limit_bytes=8 * 2**20),
    )(*args)


def finish_kernel(got_ref, longer_ref, start_ref, r0, o0, r1, o1, r2, o2, out_ref, state):
    step = pl.program_id(0)

    @pl.when(step == 0)
    def _():
        offset = jnp.where(group_here() >= 4, got_ref[...], 0.0)
        before = longer_ref[...]
        first = dot4(split(before[:, :N]), split(offset)) + before[:, N:]
        parts = split(first)
        state[0] = jnp.concatenate(parts, axis=0)
        for s in range(1, SPANS):
            pair = start_ref[s]
            state[s] = jnp.concatenate(
                split(dot4(split(pair[:, :N]), parts) + pair[:, N:]), axis=0
            )

    rhs = state[step]
    core = core_here()

    def write(place, r_ref, o_ref):
        for b in range(PAIRS):
            out = dot4(halves(r_ref[b]), (rhs[:N], rhs[N:])) + o_ref[b]
            out_ref[b, place] = out.astype(BF16)

    write(core, r0, o0)

    @pl.when(step < SPANS // 2)
    def _():
        write(1 - core, r1, o1)

    @pl.when(step >= SPANS // 2)
    def _():
        write(1 - core, r2, o2)


def finish(got, longer, start, parts):
    half = SPANS // 2

    def pieces(index):
        return [
            pl.BlockSpec((PAIRS, N, 2 * N), lambda i: (index(i), 0, 0)),
            pl.BlockSpec((PAIRS, N, N), lambda i: (index(i), 0, 0)),
        ]

    return pl.pallas_call(
        finish_kernel,
        grid=(SPANS,),
        in_specs=[
            pl.BlockSpec((N, N), lambda i: (0, 0)),
            pl.BlockSpec((N, 2 * N), lambda i: (0, 0)),
            pl.BlockSpec((SPANS, N, 2 * N), lambda i: (0, 0, 0)),
        ]
        + pieces(lambda i: i)
        + pieces(lambda i: jnp.minimum(i, half - 1))
        + pieces(lambda i: jnp.maximum(i - half, 0)),
        out_specs=spec(PAIRS, 2, N, N),
        out_shape=jax.ShapeDtypeStruct((CHIPS, 2, N, N), BF16),
        scratch_shapes=[pltpu.VMEM((SPANS, 2 * N, N), BF16)],
        compiler_params=params(16),
        cost_estimate=cost(10**9, 5),
        name="finish",
    )(got, longer, start, *parts)


PACKSTEP = 64


def pack_kernel(k_ref, q_ref, beta_ref, gate_ref, out_ref, wide):
    step = pl.program_id(0)
    for start, ref in ((0, k_ref), (Q0, q_ref)):
        wide[start // N] = ref[...].astype(F32).reshape(16 * PACKSTEP, N)
        row = pl.multiple_of(start + step * PACKSTEP, PACKSTEP)
        for h in range(16):
            rows = wide[start // N, pl.ds(h, PACKSTEP, stride=16), :]
            out_ref[h, pl.ds(row, PACKSTEP), :] = rows.astype(BF16)

    @pl.when(step == 0)
    def _():
        beta, gate = beta_ref[...].astype(F32), gate_ref[...].astype(F32)
        for h in range(16):
            pair = slice(2 * h, 2 * h + 2)
            tail = jnp.concatenate([beta[pair], gate[pair], jnp.zeros((12, N), F32)], axis=0)
            out_ref[h, G0:] = tail.astype(BF16)


def pack(key_rows, query_rows, beta_rows, log_gate):
    return pl.pallas_call(
        pack_kernel,
        grid=(N // PACKSTEP,),
        in_specs=[spec(PACKSTEP, 16, N)] * 2 + [pl.BlockSpec((32, N), lambda i: (0, 0))] * 2,
        out_specs=pl.BlockSpec((CHIPS, KROWS, N), lambda i: (0, 0, 0)),
        out_shape=jax.ShapeDtypeStruct((CHIPS, KROWS, N), BF16),
        scratch_shapes=[pltpu.VMEM((2, 16 * PACKSTEP, N), F32)],
        compiler_params=params(60),
        name="pack",
    )(key_rows, query_rows, beta_rows.T, log_gate.T)


EVERY = [list(range(32 * g, 32 * g + 32)) for g in range(8)]
ALIKE = [list(range(32 * g + core, 32 * g + 32, 2)) for g in range(8) for core in range(2)]


def exchange(x, groups):
    return lax.all_to_all(x, ("ctx", "head"), 0, 0, tiled=True, axis_index_groups=groups)


def onward(x, groups):
    ring = [(i, (i + 4 * groups) % 32) for i in range(32)]
    return lax.ppermute(x, "ctx", ring)


def other_core(x):
    return lax.ppermute(x, "head", [(i, i ^ 1) for i in range(8)])


def local(query_rows, key_rows, value_rows, beta_rows, log_gate):
    x0 = exchange(pack(key_rows, query_rows, beta_rows, log_gate), ALIKE)
    values, x0 = lax.optimization_barrier((value_rows.transpose(1, 0, 2), x0))
    x1 = other_core(x0)
    v = exchange(values, EVERY)
    aux, w, tu, m, a = solve(x0, x1)
    ph, start, total = chain(m, a, v)
    hold = lax.optimization_barrier
    made = (v, aux, w, tu, ph)
    half = CHIPS // 2
    got, part1 = hold((onward(total, 1), rows(1, 0, half, x1, *made)))
    before, run = joined(first_join_kernel, (2 * N, 2 * N), got, total)
    x0, run = hold((x0, run))
    got, part0 = hold((onward(run, 2), rows(0, 0, CHIPS, x0, *made)))
    longer, offset = joined(second_join_kernel, (2 * N, N), got, before, run)
    x1, offset = hold((x1, offset))
    part2 = rows(1, half, half, x1, *made)
    out = finish(onward(offset, 4), longer, start, [*part0, *part1, *part2])
    return exchange(out.reshape(2 * CHIPS, N, N), EVERY).transpose(1, 0, 2)


def solution(mesh):
    placed = (
        P(("ctx", "head"), None, None),
        P(("ctx", "head"), None, None),
        P(("ctx", "head"), None, None),
        P(("ctx", "head"), None),
        P(("ctx", "head"), None),
    )
    return jax.shard_map(
        local, mesh=mesh, in_specs=placed, out_specs=P(("ctx", "head"), None, None), check_vma=False
    )
```

```python
import functools

import jax
import jax.numpy as jnp
from jax import lax
from jax.experimental import pallas as pl
from jax.experimental.pallas import tpu as pltpu
from jax.sharding import PartitionSpec as P

N = 128
CHIPS = 16
SPANS = 4
PAIRS = 4
G0 = N
VROWS = N + N // 2
KROWS = N + 16
F32, BF16 = jnp.float32, jnp.bfloat16


def iota(shape, dim):
    return lax.broadcasted_iota(jnp.int32, shape, dim)


def split(x):
    hi = x.astype(BF16)
    return hi, (x - hi.astype(F32)).astype(BF16)


def dot(a, b):
    return jnp.dot(a, b, preferred_element_type=F32)


def dot_nt(a, b):
    return lax.dot_general(a, b, (((1,), (1,)), ((), ())), preferred_element_type=F32)


def dot_tn(a, b):
    return lax.dot_general(a, b, (((0,), (0,)), ((), ())), preferred_element_type=F32)


def dot_stacked(stacked, b):
    rows = stacked.shape[0] // 2
    both = dot(stacked, b)
    return both[:rows] + both[rows:]


def stack(parts):
    return jnp.concatenate(parts, axis=0)


def dot3(a, b):
    return dot_stacked(stack(a), b[0]) + dot(a[0], b[1])


def dot4(a, b):
    wide = jnp.concatenate([a[0], a[1], a[0], a[1]], axis=1)
    return dot(wide, jnp.concatenate([b[0], b[0], b[1], b[1]], axis=0))


def halves(x):
    return x[:, :N], x[:, N:]


def gate_rows(gates):
    upper = (iota((N, N), 0) <= iota((N, N), 1)).astype(F32).astype(BF16)
    return dot(gates, upper)


def gate_columns(gates):
    lower = (iota((N, N), 0) >= iota((N, N), 1)).astype(F32).astype(BF16)
    eye = (iota((N, N), 0) == iota((N, N), 1)).astype(F32).astype(BF16)
    both = dot_nt(jnp.concatenate([lower, eye], axis=0), gates)
    return both[:N], both[N:]


def small_inverses(lower_parts):
    count = len(lower_parts)
    group = iota((16, N), 1) // 16
    rows = []
    for part in lower_parts:
        packed = jnp.zeros((16, N), F32)
        for b in range(8):
            packed = jnp.where(group == b, part[16 * b : 16 * b + 16], packed)
        rows.append(packed)
    packed = jnp.concatenate(rows, axis=0)
    lane = iota((16 * count, N), 1)
    result = (lane % 16 == iota((16 * count, N), 0) % 16).astype(F32).reshape(count, 16, N)
    for j in range(15):
        factor = jnp.take_along_axis(packed, lane // 16 * 16 + j, axis=1).reshape(count, 16, N)
        result = result - factor * result[:, j : j + 1, :]
    return [
        jnp.concatenate([jnp.where(group == b, result[c], 0.0) for b in range(8)], axis=0)
        for c in range(count)
    ]


def merge(parts, lower_part, size):
    starts = range(size, N, 2 * size)

    def pick(x):
        return jnp.concatenate([x[s : s + size] for s in starts], axis=0)

    half = (N // 2, N)
    link = jnp.where(iota(half, 1) // size == 2 * (iota(half, 0) // size), pick(lower_part), 0.0)
    linked = split(dot3(split(link), parts[1:]))

    def spread(x):
        zero = jnp.zeros((size, N), BF16)
        pieces = []
        for p in range(len(starts)):
            pieces += [zero, x[p * size : (p + 1) * size]]
        return jnp.concatenate(pieces, axis=0)

    picked = [pick(x) for x in parts]
    new = picked[0] - dot3(picked[1:], (spread(linked[0]), spread(linked[1])))

    def renew(old, fresh):
        pieces = []
        for p, s in enumerate(starts):
            pieces += [old[s - size : s], fresh[p * size : (p + 1) * size]]
        return jnp.concatenate(pieces, axis=0)

    return [renew(old, fresh) for old, fresh in zip(parts, (new,) + split(new))]


def params(megabytes):
    return pltpu.CompilerParams(
        dimension_semantics=("arbitrary",), vmem_limit_bytes=megabytes * 2**20
    )


def cost(flops, megabytes):
    return pl.CostEstimate(flops=flops, bytes_accessed=megabytes * 2**20, transcendentals=10**6)


def in_hbm(*arrays):
    return [pltpu.with_memory_space_constraint(x, pltpu.HBM) for x in arrays]


def core_here():
    return lax.axis_index("head") % 2


def group_here():
    return lax.axis_index("ctx") // 4


def spec(*shape):
    return pl.BlockSpec(shape, lambda i: (i,) + (0,) * (len(shape) - 1))


STEP = 16


def solve_kernel(x0_ref, x1_ref, aux_ref, w_ref, tu_ref, m_ref, a_ref):
    first = core_here() == 0
    units = [(x_ref, b, which) for which, x_ref in enumerate((x0_ref, x1_ref)) for b in range(STEP)]
    eye = iota((N, N), 0) == iota((N, N), 1)
    strict = iota((N, N), 0) > iota((N, N), 1)
    lower_parts, scales = [], []
    for x_ref, b, which in units:
        key = x_ref[b, :N]
        gates = x_ref[b, G0 : G0 + 16]
        rows_here = gate_rows(gates)
        cols_here, beta_cols = gate_columns(gates)
        wide = gates.astype(F32)
        brow = jnp.where(first, wide[0:1], wide[1:2])
        bcol = jnp.where(first, beta_cols[:, 0:1], beta_cols[:, 1:2])
        crow = jnp.where(first, rows_here[2:3], rows_here[3:4])
        ccol = jnp.where(first, cols_here[:, 2:3], cols_here[:, 3:4])
        gram = dot_nt(key, key)
        diagonal = jnp.where(eye, gram, 0.0)
        norm_row = lax.rsqrt(jnp.sum(diagonal, axis=0, keepdims=True) + 1e-06)
        norm_col = lax.rsqrt(jnp.sum(diagonal, axis=1, keepdims=True) + 1e-06)
        decay = jnp.exp(jnp.minimum(ccol - crow, 0.0))
        scaled = gram * (norm_col * bcol) * norm_row * decay
        lower_parts.append(jnp.where(strict, scaled, 0.0))
        last = crow[:, N - 1 : N]
        scales.append((
            brow * jnp.exp(crow) * norm_row,
            brow,
            norm_col * jnp.exp(last - ccol),
            jnp.exp(last),
        ))
        aux_ref[b, which] = jnp.concatenate([crow, norm_row, jnp.zeros((6, N), F32)], axis=0)
    inverses = [(t,) + split(t) for t in small_inverses(lower_parts)]
    for size in (16, 32, 64):
        inverses = [merge(t, g, size) for t, g in zip(inverses, lower_parts)]
    inverses = [t[0] for t in inverses]
    for inverse, (for_w, for_u, for_state, last), (x_ref, b, which) in zip(inverses, scales, units):
        key = x_ref[b, :N]
        w = dot_stacked(stack(split(inverse * for_w)), key)
        tu = inverse * for_u
        tu_ref[b, which] = stack(split(tu))
        w_ref[b, which] = w
        hi, lo = split(jnp.concatenate([w, tu], axis=1) * for_state)
        both = dot_tn(key, hi) + dot_tn(key, lo)
        a_ref[b, which] = jnp.concatenate(split(jnp.where(eye, last, 0.0) - both[:, :N]), axis=1)
        m_ref[b, which] = stack(split(both[:, N:]))


def solve(x0, x1):
    return pl.pallas_call(
        solve_kernel,
        grid=(CHIPS // STEP,),
        in_specs=[spec(STEP, KROWS, N)] * 2,
        out_specs=[spec(STEP, 2, 8, N), spec(STEP, 2, N, N)] + [spec(STEP, 2, 2 * N, N)] * 2 + [spec(STEP, 2, N, 2 * N)],
        out_shape=[
            pltpu.HBM((CHIPS, 2, 8, N), F32),
            pltpu.HBM((CHIPS, 2, N, N), F32),
        ]
        + [pltpu.HBM((CHIPS, 2, 2 * N, N), BF16)] * 2
        + [pltpu.HBM((CHIPS, 2, N, 2 * N), BF16)],
        compiler_params=params(24),
        cost_estimate=cost(16 * 10**9, 20),
        name="solve",
    )(x0, x1)


def later(a, offset, parts):
    moved = dot4(a, parts)
    return jnp.concatenate([moved[:, :N], moved[:, N:] + offset], axis=1)


def unit_pair():
    return jnp.where(iota((N, 2 * N), 0) == iota((N, 2 * N), 1), 1.0, 0.0)


def chain_kernel(m_ref, a_ref, v_ref, ph_ref, start_ref, total_ref, state):
    step = pl.program_id(0)

    @pl.when(step == 0)
    def _():
        for s in range(SPANS):
            state[s] = unit_pair()

    def advance(order):
        for place, which in enumerate(order):
            for s in range(SPANS):
                value = v_ref[s, 0, place, :N]
                offset = dot_stacked(m_ref[s, 0, which], value)
                parts = split(state[s])
                ph_ref[s, 0, which] = jnp.concatenate(parts, axis=0)
                state[s] = later(halves(a_ref[s, 0, which]), offset, parts)

    @pl.when(core_here() == 0)
    def _():
        advance((0, 1))

    @pl.when(core_here() != 0)
    def _():
        advance((1, 0))

    @pl.when(step == PAIRS - 1)
    def _():
        running = state[0]
        start_ref[0] = unit_pair()
        for s in range(1, SPANS):
            start_ref[s] = running
            running = later(split(state[s, :, :N]), state[s, :, N:], split(running))
        total_ref[...] = running


def chain(m, a, v):
    def of_pair(*shape):
        return pl.BlockSpec((SPANS, 1) + shape, lambda i: (0, i) + (0,) * len(shape))

    m, a = m.reshape(SPANS, PAIRS, 2, 2 * N, N), a.reshape(SPANS, PAIRS, 2, N, 2 * N)
    return pl.pallas_call(
        chain_kernel,
        grid=(PAIRS,),
        in_specs=[of_pair(2, 2 * N, N), of_pair(2, N, 2 * N), of_pair(2, VROWS, N)],
        out_specs=[
            of_pair(2, 2 * N, 2 * N),
            pl.BlockSpec((SPANS, N, 2 * N), lambda i: (0, 0, 0)),
            pl.BlockSpec((N, 2 * N), lambda i: (0, 0)),
        ],
        out_shape=[
            jax.ShapeDtypeStruct((SPANS, PAIRS, 2, 2 * N, 2 * N), BF16),
            jax.ShapeDtypeStruct((SPANS, N, 2 * N), F32),
            jax.ShapeDtypeStruct((N, 2 * N), F32),
        ],
        scratch_shapes=[pltpu.VMEM((SPANS, N, 2 * N), F32)],
        compiler_params=params(16),
        cost_estimate=cost(4 * 10**9, 10),
        name="chain",
    )(*in_hbm(m, a), v.reshape(SPANS, PAIRS, 2, VROWS, N))


PRESTEP = 4
ROWSTEP = 8


def before_queries_kernel(v_ref, w_ref, tu_ref, ph_ref, e_ref):
    core = core_here()
    for b in range(PRESTEP):
        for which in range(2):
            value = v_ref[b, core if which == 0 else 1 - core, :N]
            u = dot_stacked(tu_ref[b, which], value)
            ph = ph_ref[b, which]
            moved = dot4(split(w_ref[b, which]), (ph[:N], ph[N:]))
            errors = jnp.concatenate([-moved[:, :N], u - moved[:, N:]], axis=1)
            e_ref[b, which] = stack(split(errors))


def before_queries(first, count, v, w, tu, ph):
    def some(*shape):
        return pl.BlockSpec(
            (PRESTEP, 2) + shape, lambda i: (first // PRESTEP + i,) + (0,) * (len(shape) + 1)
        )

    return pl.pallas_call(
        before_queries_kernel,
        grid=(count // PRESTEP,),
        in_specs=[some(VROWS, N), some(N, N), some(2 * N, N), some(2 * N, 2 * N)],
        out_specs=spec(PRESTEP, 2, 2 * N, 2 * N),
        out_shape=jax.ShapeDtypeStruct((count, 2, 2 * N, 2 * N), BF16),
        compiler_params=params(20),
        cost_estimate=cost(count * 3 * 10**8, count // 2),
        name="before_queries",
    )(v.reshape(CHIPS, 2, VROWS, N), w, tu, ph)


def rows_kernel(which, x_ref, v_ref, q_ref, aux_ref, e_ref, ph_ref, r_ref, o_ref):
    core = core_here()
    first = core == 0
    place = core if which == 0 else 1 - core
    inclusive = iota((N, N), 0) >= iota((N, N), 1)
    for b in range(ROWSTEP):
        key = x_ref[b, :N]
        here, there = v_ref[b, place, N:].astype(F32), q_ref[b, place].astype(F32)
        wide = jnp.concatenate(
            [jnp.where(first, here, there), jnp.where(first, there, here)], axis=0
        )
        query = wide.astype(BF16)
        cols_here, _ = gate_columns(x_ref[b, G0 : G0 + 16])
        ccol = jnp.where(first, cols_here[:, 2:3], cols_here[:, 3:4])
        norm = lax.rsqrt(jnp.sum(wide * wide, axis=1, keepdims=True) + 1e-06) * N ** (-0.5)
        decay = jnp.exp(jnp.minimum(ccol - aux_ref[b, 0:1], 0.0))
        scores = dot_nt(query, key) * norm * aux_ref[b, 1:2] * decay
        scores = jnp.where(inclusive, scores, 0.0)
        carried = dot(jnp.concatenate([query, query], axis=1), ph_ref[b])
        both = dot4(split(scores), (e_ref[b, :N], e_ref[b, N:])) + carried * (norm * jnp.exp(ccol))
        r_ref[b] = jnp.concatenate(split(both[:, :N]), axis=1)
        o_ref[b] = both[:, N:]


def rows(which, x, v, q, aux, e, ph):
    first, count = 0, CHIPS

    def some(*shape):
        return pl.BlockSpec((ROWSTEP,) + shape, lambda i: (first // ROWSTEP + i,) + (0,) * len(shape))

    def one_of(start, *shape):
        return pl.BlockSpec(
            (ROWSTEP, None) + shape,
            lambda i: (start // ROWSTEP + i, which) + (0,) * len(shape),
        )

    return pl.pallas_call(
        functools.partial(rows_kernel, which),
        grid=(count // ROWSTEP,),
        in_specs=[
            some(KROWS, N),
            some(2, VROWS, N),
            some(2, N // 2, N),
            one_of(first, 8, N),
            one_of(0, 2 * N, 2 * N),
            one_of(first, 2 * N, 2 * N),
        ],
        out_specs=[spec(ROWSTEP, N, 2 * N), spec(ROWSTEP, N, N)],
        out_shape=[
            jax.ShapeDtypeStruct((count, N, 2 * N), BF16),
            jax.ShapeDtypeStruct((count, N, N), F32),
        ],
        compiler_params=params(20),
        cost_estimate=cost(count * 3 * 10**8, count // 2),
        name="rows",
    )(x, v.reshape(CHIPS, 2, VROWS, N), q.reshape(CHIPS, 2, N // 2, N), aux, e, ph)


def first_join_kernel(got_ref, own_ref, before_ref, run_ref):
    before = jnp.where(group_here() >= 1, got_ref[...], unit_pair())
    own = own_ref[...]
    before_ref[...] = before
    run_ref[...] = later(split(own[:, :N]), own[:, N:], split(before))


def second_join_kernel(got_ref, before_ref, run_ref, longer_ref, offset_ref):
    got = split(jnp.where(group_here() >= 2, got_ref[...], unit_pair()))
    run, before = run_ref[...], before_ref[...]
    offset_ref[...] = dot4(split(run[:, :N]), (got[0][:, N:], got[1][:, N:])) + run[:, N:]
    longer_ref[...] = later(split(before[:, :N]), before[:, N:], got)


def joined(kernel, outs, *args):
    vmem = pl.BlockSpec(memory_space=pltpu.VMEM)
    return pl.pallas_call(
        kernel,
        in_specs=[vmem] * len(args),
        out_shape=[jax.ShapeDtypeStruct((N, width), F32) for width in outs],
        compiler_params=pltpu.CompilerParams(vmem_limit_bytes=8 * 2**20),
    )(*args)


def finish_kernel(got_ref, longer_ref, start_ref, r0, o0, r1, o1, out_ref, state):
    step = pl.program_id(0)

    @pl.when(step == 0)
    def _():
        offset = jnp.where(group_here() >= 4, got_ref[...], 0.0)
        before = longer_ref[...]
        first = dot4(split(before[:, :N]), split(offset)) + before[:, N:]
        parts = split(first)
        state[0] = jnp.concatenate(parts, axis=0)
        for s in range(1, SPANS):
            pair = start_ref[s]
            state[s] = jnp.concatenate(
                split(dot4(split(pair[:, :N]), parts) + pair[:, N:]), axis=0
            )

    rhs = state[step]
    core = core_here()

    def write(place, r_ref, o_ref):
        for b in range(PAIRS):
            out = dot4(halves(r_ref[b]), (rhs[:N], rhs[N:])) + o_ref[b]
            out_ref[b, place] = out.astype(BF16)

    write(core, r0, o0)
    write(1 - core, r1, o1)


def finish(got, longer, start, parts):
    return pl.pallas_call(
        finish_kernel,
        grid=(SPANS,),
        in_specs=[
            pl.BlockSpec((N, N), lambda i: (0, 0)),
            pl.BlockSpec((N, 2 * N), lambda i: (0, 0)),
            pl.BlockSpec((SPANS, N, 2 * N), lambda i: (0, 0, 0)),
        ]
        + 2 * [spec(PAIRS, N, 2 * N), spec(PAIRS, N, N)],
        out_specs=spec(PAIRS, 2, N, N),
        out_shape=jax.ShapeDtypeStruct((CHIPS, 2, N, N), BF16),
        scratch_shapes=[pltpu.VMEM((SPANS, 2 * N, N), BF16)],
        compiler_params=params(16),
        cost_estimate=cost(10**9, 5),
        name="finish",
    )(got, longer, start, *parts)


PACKSTEP = 64


def pack_kernel(k_ref, beta_ref, gate_ref, out_ref, wide):
    step = pl.program_id(0)
    wide[...] = k_ref[...].astype(F32).reshape(16 * PACKSTEP, N)
    row = pl.multiple_of(step * PACKSTEP, PACKSTEP)
    for h in range(16):
        rows = wide[pl.ds(h, PACKSTEP, stride=16), :]
        out_ref[h, pl.ds(row, PACKSTEP), :] = rows.astype(BF16)

    @pl.when(step == 0)
    def _():
        beta, gate = beta_ref[...].astype(F32), gate_ref[...].astype(F32)
        for h in range(16):
            pair = slice(2 * h, 2 * h + 2)
            tail = jnp.concatenate([beta[pair], gate[pair], jnp.zeros((12, N), F32)], axis=0)
            out_ref[h, G0:] = tail.astype(BF16)


def pack(key_rows, beta_rows, log_gate):
    return pl.pallas_call(
        pack_kernel,
        grid=(N // PACKSTEP,),
        in_specs=[spec(PACKSTEP, 16, N)] + [pl.BlockSpec((32, N), lambda i: (0, 0))] * 2,
        out_specs=pl.BlockSpec((CHIPS, KROWS, N), lambda i: (0, 0, 0)),
        out_shape=jax.ShapeDtypeStruct((CHIPS, KROWS, N), BF16),
        scratch_shapes=[pltpu.VMEM((16 * PACKSTEP, N), F32)],
        compiler_params=params(60),
        name="pack",
    )(key_rows, beta_rows.T, log_gate.T)


EVERY = [list(range(32 * g, 32 * g + 32)) for g in range(8)]
ALIKE = [list(range(32 * g + core, 32 * g + 32, 2)) for g in range(8) for core in range(2)]


def exchange(x, groups):
    return lax.all_to_all(x, ("ctx", "head"), 0, 0, tiled=True, axis_index_groups=groups)


def onward(x, groups):
    ring = [(i, (i + 4 * groups) % 32) for i in range(32)]
    return lax.ppermute(x, "ctx", ring)


def other_core(x):
    return lax.ppermute(x, "head", [(i, i ^ 1) for i in range(8)])


def local(query_rows, key_rows, value_rows, beta_rows, log_gate):
    hold = lax.optimization_barrier
    x0 = exchange(pack(key_rows, beta_rows, log_gate), ALIKE)
    halved = query_rows.transpose(1, 0, 2).reshape(2 * CHIPS, N // 2, N)
    values = jnp.concatenate([value_rows.transpose(1, 0, 2), halved], axis=1)
    values, x0 = hold((values, x0))
    x1 = other_core(x0)
    v = exchange(values, EVERY)
    aux, w, tu, m, a = solve(x0, x1)
    ph, start, total = chain(m, a, v)
    ph = ph.reshape(CHIPS, 2, 2 * N, 2 * N)
    q = other_core(v[:, N:])
    got, e = hold((onward(total, 1), before_queries(0, CHIPS, v, w, tu, ph)))
    before, run = joined(first_join_kernel, (2 * N, 2 * N), got, total)
    x0, run = hold((x0, run))
    got, part0 = hold((onward(run, 2), rows(0, x0, v, q, aux, e, ph)))
    longer, offset = joined(second_join_kernel, (2 * N, N), got, before, run)
    x1, offset = hold((x1, offset))
    part1 = rows(1, x1, v, q, aux, e, ph)
    out = finish(onward(offset, 4), longer, start, [*part0, *part1])
    return exchange(out.reshape(2 * CHIPS, N, N), EVERY).transpose(1, 0, 2)


def solution(mesh):
    placed = (
        P(("ctx", "head"), None, None),
        P(("ctx", "head"), None, None),
        P(("ctx", "head"), None, None),
        P(("ctx", "head"), None),
        P(("ctx", "head"), None),
    )
    return jax.shard_map(
        local, mesh=mesh, in_specs=placed, out_specs=P(("ctx", "head"), None, None), check_vma=False
    )
```
